512 devices in a mesh: rows: 8 (over z), cols: 8 (over y), depth: 8 (over x, core).
Axes of the slice: x: 4, y: 8, z: 8, core: 2. Of those that a mesh axis runs over, the one named last changes fastest.
Arguments:
- tokens: bfloat16 [512, 12288], P(('rows', 'cols'), 'depth'), may hold values from -6 to 6
- weight_in: bfloat16 [12288, 49152], P('depth', ('rows', 'cols')), may hold values from -0.0546875 to 0.0546875
- bias_in: float32 [49152], P(('rows', 'cols')), may hold values from -4 to 4
- weight_out: bfloat16 [49152, 12288], P(('rows', 'cols'), 'depth'), may hold values from -0.02734375 to 0.02734375
- bias_out: float32 [12288], P('depth'), may hold values from -3 to 3
Outputs:
- output: bfloat16 [512, 12288], P(('rows', 'cols'), 'depth')
The draws below stay inside these ranges and needn't reach their ends.
All inputs are finite; a program needn't handle non-finite values.
Results may differ from the reference program's by a relative error of at most 0.0046.
Values may be sent and summed in bfloat16 or wider, within the bound.
No kernel may reach another device: no remote copies, remote signals or barrier semaphores. Data moves between devices by JAX's collectives and lax.ppermute only.
A program may use at most 64 MiB of HBM per device.

```python
import jax
import jax.numpy as jnp

D = 12288
F = 49152
TOKENS = 512


def shard_levels(stream_key, shape, pieces, low, top_value):
    def one(axis_at, parts):
        heights = jax.random.uniform(jax.random.fold_in(jax.random.fold_in(stream_key, 6), axis_at), (parts,), jnp.float32, low / len(pieces), top_value / len(pieces))
        return jnp.repeat(jnp.exp(heights), shape[axis_at] // parts).reshape((-1,) + (1,) * (len(shape) - axis_at - 1))

    gain = one(*pieces[0])
    for cut in pieces[1:]:
        gain = gain * one(*cut)
    return gain


def normal_values(rng, dims, deviation, reach, shards=(), held_as=jnp.bfloat16):
    loudness = shard_levels(rng, dims, shards, -0.22, 0.18) if shards else 1.0
    entries = jax.random.normal(rng, dims, jnp.float32) * deviation * loudness
    return jnp.minimum(jnp.maximum(entries, -reach), reach).astype(held_as)


def setup_inputs(seed: int = 0) -> dict:
    key_of = jax.random.split(jax.random.key(seed), 6)
    tokens = normal_values(key_of[0], (TOKENS, D), 1.0, 6.0, ((0, 64), (1, 8)))
    weight_in = normal_values(key_of[1], (D, F), D ** -0.5, 0.0546875, ((0, 8), (1, 64)))
    bias_in = normal_values(key_of[2], (F,), 1.0, 4.0, ((0, 64),), jnp.float32)
    weight_out = normal_values(key_of[3], (F, D), F ** -0.5, 0.02734375, ((0, 64), (1, 8)))
    bias_out = normal_values(key_of[4], (D,), 0.5, 3.0, ((0, 8),), jnp.float32)
    return {"tokens": tokens, "weight_in": weight_in, "bias_in": bias_in, "weight_out": weight_out, "bias_out": bias_out}


def reference(tokens, weight_in, bias_in, weight_out, bias_out):
    hidden = jnp.dot(tokens, weight_in, preferred_element_type=jnp.float32) + bias_in.astype(jnp.float32)
    active = jax.nn.gelu(hidden, approximate=True).astype(jnp.bfloat16)
    summed = jnp.dot(active, weight_out, preferred_element_type=jnp.float32) + bias_out.astype(jnp.float32)
    return summed.astype(jnp.bfloat16)
```

```python
import jax
import jax.numpy as jnp
from jax import lax
from jax.sharding import PartitionSpec as P

PLANE = ("rows", "cols")


def shards(tokens, weight_in, bias_in, weight_out, bias_out):
    own = tokens.shape[0]
    planes = lax.axis_size(PLANE)
    gathered = lax.all_to_all(
        jnp.broadcast_to(tokens[None], (planes,) + tokens.shape), PLANE, 0, 0
    ).reshape(planes * own, -1)
    partial_hidden = jnp.dot(gathered, weight_in, preferred_element_type=jnp.float32)
    depths = lax.axis_size("depth")
    pieces = lax.all_to_all(
        partial_hidden.astype(jnp.bfloat16).reshape(depths, -1, weight_in.shape[1]),
        "depth", 0, 0,
    )
    hidden = jnp.sum(pieces.astype(jnp.float32), axis=0) + bias_in
    active = jax.nn.gelu(hidden, approximate=True).astype(jnp.bfloat16)
    active = lax.all_gather(active, "depth", axis=0, tiled=True)
    partial_out = jnp.dot(active, weight_out, preferred_element_type=jnp.float32)
    parts = lax.all_to_all(
        partial_out.astype(jnp.bfloat16).reshape(planes, own, -1), PLANE, 0, 0
    )
    summed = jnp.sum(parts.astype(jnp.float32), axis=0)
    return (summed + bias_out).astype(jnp.bfloat16)


def solution(mesh):
    in_specs = (
        P(("rows", "cols"), "depth"),
        P("depth", ("rows", "cols")),
        P(("rows", "cols")),
        P(("rows", "cols"), "depth"),
        P("depth"),
    )
    out_specs = P(("rows", "cols"), "depth")
    return jax.shard_map(shards, mesh=mesh, in_specs=in_specs, out_specs=out_specs, check_vma=False)
```

```python
import jax
import jax.numpy as jnp
from jax import lax
from jax.sharding import PartitionSpec as P

PLANE = ("rows", "cols")
ALL = ("rows", "cols", "depth")


def parity_groups(n_rows, n_cols):
    return [
        [r * n_cols + c for r in range(p, n_rows, 2) for c in range(q, n_cols, 2)]
        for p in range(2)
        for q in range(2)
    ]


def square_groups(n_rows, n_cols, n_depth):
    groups = []
    for d in range(n_depth):
        for r in range(d % 2, n_rows + d % 2, 2):
            for c in range(d % 2, n_cols + d % 2, 2):
                chips = [(i % n_rows, j % n_cols) for i in (r, r + 1) for j in (c, c + 1)]
                chips.sort(key=lambda chip: (chip[0] % 2, chip[1] % 2))
                groups.append([(i * n_cols + j) * n_depth + d for i, j in chips])
    return groups


def swap_cores(x):
    return lax.ppermute(x, "depth", [(d, d ^ 1) for d in range(lax.axis_size("depth"))])


def swap_chips(x, stage):
    n = lax.axis_size("depth")
    pairs = []
    for d in range(n):
        chip, core = d // 2, d % 2
        step = 1 if (chip + core + stage) % 2 == 0 else -1
        pairs.append((d, ((chip + step) * 2 + core) % n))
    return lax.ppermute(x, "depth", pairs)


def shards(tokens, weight_in, bias_in, weight_out, bias_out):
    own, width = tokens.shape
    n_rows, n_cols, n_depth = (lax.axis_size(a) for a in ALL)
    far, near = parity_groups(n_rows, n_cols), square_groups(n_rows, n_cols, n_depth)
    members = n_rows * n_cols // 4
    quarter = members * own
    f32, bf16 = jnp.float32, jnp.bfloat16
    first = lax.axis_index("depth") % 2 == 0
    tokens, first = lax.optimization_barrier((tokens, first))

    def repeat(x, n):
        return jnp.broadcast_to(x[None], (n,) + x.shape)

    def add(x):
        x = x.astype(f32)
        return (x[0] + x[1]) + (x[2] + x[3])

    mine = lax.all_to_all(repeat(tokens, members), PLANE, 0, 0, axis_index_groups=far).reshape(quarter, width)
    full = lax.all_to_all(repeat(mine, 4), ALL, 0, 0, axis_index_groups=near).reshape(-1, width)
    partial = jnp.dot(full, weight_in, preferred_element_type=f32)

    partial = partial.reshape(4, 2, quarter // 2, -1)
    keep = jnp.where(first, partial[:, 0], partial[:, 1])
    send = jnp.where(first, partial[:, 1], partial[:, 0])
    total = keep + swap_cores(send)
    for stage in range(2):
        total = total + swap_chips(total.astype(bf16), stage).astype(f32)
    ours = jax.nn.gelu(total + bias_in, approximate=True).astype(bf16)
    theirs = swap_cores(ours)
    active = jnp.stack([jnp.where(first, ours, theirs), jnp.where(first, theirs, ours)], axis=1)
    active = active.reshape(4 * quarter, -1)

    outs = jnp.dot(active, weight_out, preferred_element_type=f32).astype(bf16)
    total = add(lax.all_to_all(outs.reshape(4, quarter, width), ALL, 0, 0, axis_index_groups=near))
    parts = lax.all_to_all(total.astype(bf16).reshape(members, own, width), PLANE, 0, 0, axis_index_groups=far)
    return (jnp.sum(parts.astype(f32), axis=0) + bias_out).astype(bf16)


def solution(mesh):
    in_specs = (
        P(("rows", "cols"), "depth"),
        P("depth", ("rows", "cols")),
        P(("rows", "cols")),
        P(("rows", "cols"), "depth"),
        P("depth"),
    )
    out_specs = P(("rows", "cols"), "depth")
    return jax.shard_map(shards, mesh=mesh, in_specs=in_specs, out_specs=out_specs, check_vma=False)
```

```python
import jax
import jax.numpy as jnp
from jax import lax
from jax.sharding import PartitionSpec as P

ALL = ("rows", "cols", "depth")


def parity_groups(n_rows, n_cols, n_depth):
    groups = []
    for d in range(n_depth):
        for p in range(2):
            for q in range(2):
                chips = [r * n_cols + c for r in range(p, n_rows, 2) for c in range(q, n_cols, 2)]
                half = len(chips) // 2 * (d % 2)
                groups.append([chip * n_depth + d for chip in chips[half:] + chips[:half]])
    return groups


def square_groups(n_rows, n_cols, n_depth):
    groups = []
    for d in range(n_depth):
        for r in range(d % 2, n_rows + d % 2, 2):
            for c in range(1 - d % 2, n_cols + 1 - d % 2, 2):
                chips = [(i % n_rows, j % n_cols) for i in (r, r + 1) for j in (c, c + 1)]
                chips.sort(key=lambda chip: (chip[0] % 2, chip[1] % 2))
                groups.append([(i * n_cols + j) * n_depth + d for i, j in chips])
    return groups


def swap_cores(x):
    return lax.ppermute(x, "depth", [(d, d ^ 1) for d in range(lax.axis_size("depth"))])


def swap_chips(x, stage):
    n = lax.axis_size("depth")
    pairs = []
    for d in range(n):
        chip, core = d // 2, d % 2
        step = 1 if (chip + core + stage) % 2 == 0 else -1
        pairs.append((d, ((chip + step) * 2 + core) % n))
    return lax.ppermute(x, "depth", pairs)


def shards(tokens, weight_in, bias_in, weight_out, bias_out):
    own, width = tokens.shape
    n_rows, n_cols, n_depth = (lax.axis_size(a) for a in ALL)
    far, near = parity_groups(n_rows, n_cols, n_depth), square_groups(n_rows, n_cols, n_depth)
    members = n_rows * n_cols // 4
    quarter = members * own
    f32, bf16 = jnp.float32, jnp.bfloat16

    def repeat(x, n):
        return jnp.broadcast_to(x[None], (n,) + x.shape)

    def add(x):
        x = x.astype(f32)
        return (x[0] + x[1]) + (x[2] + x[3])

    mine = lax.all_to_all(repeat(tokens, members), ALL, 0, 0, axis_index_groups=far).reshape(quarter, width)
    full = lax.all_to_all(repeat(mine, 4), ALL, 0, 0, axis_index_groups=near).reshape(-1, width)
    partial = jnp.dot(full, weight_in, preferred_element_type=f32)

    ours, theirs = jnp.unstack(partial.reshape(4, 2, quarter // 2, -1), axis=1)
    ours = ours + swap_cores(theirs)
    for stage in range(2):
        ours = ours + swap_chips(ours.astype(bf16), stage).astype(f32)
    ours = jax.nn.gelu(ours + bias_in, approximate=True).astype(bf16)
    active = jnp.stack([ours, swap_cores(ours)], axis=1).reshape(4 * quarter, -1)

    outs = jnp.dot(active, weight_out, preferred_element_type=f32).astype(bf16)
    total = add(lax.all_to_all(outs.reshape(4, quarter, width), ALL, 0, 0, axis_index_groups=near))
    parts = lax.all_to_all(total.astype(bf16).reshape(members, own, width), ALL, 0, 0, axis_index_groups=far)
    return (jnp.sum(parts.astype(f32), axis=0) + bias_out).astype(bf16)


def solution(mesh):
    in_specs = (
        P(("rows", "cols"), "depth"),
        P("depth", ("rows", "cols")),
        P(("rows", "cols")),
        P(("rows", "cols"), "depth"),
        P("depth"),
    )
    out_specs = P(("rows", "cols"), "depth")
    return jax.shard_map(shards, mesh=mesh, in_specs=in_specs, out_specs=out_specs, check_vma=False)
```

```python
import jax
import jax.numpy as jnp
from jax import lax
from jax.sharding import PartitionSpec as P

ALL = ("rows", "cols", "depth")


def parity_groups(n_rows, n_cols, n_depth):
    groups = []
    for d in range(n_depth):
        for p in range(2):
            for q in range(2):
                chips = [r * n_cols + c for r in range(p, n_rows, 2) for c in range(q, n_cols, 2)]
                half = len(chips) // 2 * (d % 2)
                groups.append([chip * n_depth + d for chip in chips[half:] + chips[:half]])
    return groups


def square_groups(n_rows, n_cols, n_depth):
    groups = []
    for d in range(n_depth):
        for r in range(d % 2, n_rows + d % 2, 2):
            for c in range(1 - d % 2, n_cols + 1 - d % 2, 2):
                chips = [(i % n_rows, j % n_cols) for i in (r, r + 1) for j in (c, c + 1)]
                chips.sort(key=lambda chip: (chip[0] % 2, chip[1] % 2))
                groups.append([(i * n_cols + j) * n_depth + d for i, j in chips])
    return groups


def swap_cores(x):
    return lax.ppermute(x, "depth", [(d, d ^ 1) for d in range(lax.axis_size("depth"))])


def swap_chips(x, stage):
    n = lax.axis_size("depth")
    pairs = []
    for d in range(n):
        chip, core = d // 2, d % 2
        step = 1 if (chip + core + stage) % 2 == 0 else -1
        pairs.append((d, ((chip + step) * 2 + core) % n))
    return lax.ppermute(x, "depth", pairs)


def shards(tokens, weight_in, bias_in, weight_out, bias_out):
    own, width = tokens.shape
    n_rows, n_cols, n_depth = (lax.axis_size(a) for a in ALL)
    far, near = parity_groups(n_rows, n_cols, n_depth), square_groups(n_rows, n_cols, n_depth)
    members = n_rows * n_cols // 4
    quarter = members * own
    f32, bf16 = jnp.float32, jnp.bfloat16

    def repeat(x, n):
        return jnp.broadcast_to(x[None], (n,) + x.shape)

    def add(x):
        x = x.astype(f32)
        return (x[0] + x[1]) + (x[2] + x[3])

    mine = lax.all_to_all(repeat(tokens, members), ALL, 0, 0, axis_index_groups=far).reshape(quarter, width)
    full = lax.all_to_all(repeat(mine, 4), ALL, 0, 0, axis_index_groups=near).reshape(-1, width)

    ours, theirs = jnp.unstack(full.reshape(4, 2, quarter // 2, width), axis=1)
    theirs = swap_cores(jnp.dot(theirs, weight_in, preferred_element_type=f32))
    ours = jnp.dot(ours, weight_in, preferred_element_type=f32)
    ours, theirs = lax.optimization_barrier((ours, theirs))
    ours = ours + theirs
    for stage in range(2):
        ours = ours + swap_chips(ours.astype(bf16), stage).astype(f32)
    ours = jax.nn.gelu(ours + bias_in, approximate=True).astype(bf16)
    active = [ours, swap_cores(ours)]

    outs = [jnp.dot(a, weight_out, preferred_element_type=f32).astype(bf16) for a in active]
    outs = jnp.stack(outs, axis=1)
    total = add(lax.all_to_all(outs.reshape(4, quarter, width), ALL, 0, 0, axis_index_groups=near))
    parts = lax.all_to_all(total.astype(bf16).reshape(members, own, width), ALL, 0, 0, axis_index_groups=far)
    return (jnp.sum(parts.astype(f32), axis=0) + bias_out).astype(bf16)


def solution(mesh):
    in_specs = (
        P(("rows", "cols"), "depth"),
        P("depth", ("rows", "cols")),
        P(("rows", "cols")),
        P(("rows", "cols"), "depth"),
        P("depth"),
    )
    out_specs = P(("rows", "cols"), "depth")
    return jax.shard_map(shards, mesh=mesh, in_specs=in_specs, out_specs=out_specs, check_vma=False)
```

```python
import jax
import jax.numpy as jnp
from jax import lax
from jax.sharding import PartitionSpec as P

ALL = ("rows", "cols", "depth")


def parity_groups(n_rows, n_cols, n_depth):
    groups = []
    for d in range(n_depth):
        for p in range(2):
            for q in range(2):
                chips = [r * n_cols + c for r in range(p, n_rows, 2) for c in range(q, n_cols, 2)]
                chips[len(chips) // 2 :] = chips[: len(chips) // 2 - 1 : -1]
                half = len(chips) // 2 * (d % 2)
                groups.append([chip * n_depth + d for chip in chips[half:] + chips[:half]])
    return groups


def square_groups(n_rows, n_cols, n_depth):
    groups = []
    for d in range(n_depth):
        for r in range(d % 2, n_rows + d % 2, 2):
            for c in range(1 - d % 2, n_cols + 1 - d % 2, 2):
                chips = [(i % n_rows, j % n_cols) for i in (r, r + 1) for j in (c, c + 1)]
                chips.sort(key=lambda chip: ((chip[0] + chip[1]) % 2, chip[0] % 2))
                groups.append([(i * n_cols + j) * n_depth + d for i, j in chips])
    return groups


def swap_cores(x):
    return lax.ppermute(x, "depth", [(d, d ^ 1) for d in range(lax.axis_size("depth"))])


def swap_chips(x, stage):
    n = lax.axis_size("depth")
    pairs = []
    for d in range(n):
        chip, core = d // 2, d % 2
        step = 1 if (chip + core + stage) % 2 == 0 else -1
        pairs.append((d, ((chip + step) * 2 + core) % n))
    return lax.ppermute(x, "depth", pairs)


def shards(tokens, weight_in, bias_in, weight_out, bias_out):
    own, width = tokens.shape
    n_rows, n_cols, n_depth = (lax.axis_size(a) for a in ALL)
    far, near = parity_groups(n_rows, n_cols, n_depth), square_groups(n_rows, n_cols, n_depth)
    members = n_rows * n_cols // 4
    quarter = members * own
    f32, bf16 = jnp.float32, jnp.bfloat16

    def repeat(x, n):
        return jnp.broadcast_to(x[None], (n,) + x.shape)

    def add(x):
        x = x.astype(f32)
        return (x[0] + x[1]) + (x[2] + x[3])

    mine = lax.all_to_all(repeat(tokens, members), ALL, 0, 0, axis_index_groups=far).reshape(quarter, width)
    full = lax.all_to_all(repeat(mine, 4), ALL, 0, 0, axis_index_groups=near).reshape(-1, width)

    ours, theirs = jnp.unstack(full.reshape(4, 2, quarter // 2, width), axis=1)
    theirs = swap_cores(jnp.dot(theirs, weight_in, preferred_element_type=f32))
    ours = jnp.dot(ours, weight_in, preferred_element_type=f32)
    ours, theirs = lax.optimization_barrier((ours, theirs))
    ours = ours + theirs
    for stage in range(2):
        ours = ours + swap_chips(ours.astype(bf16), stage).astype(f32)
    ours = jax.nn.gelu(ours + bias_in, approximate=True).astype(bf16)
    active = [ours, swap_cores(ours)]

    outs = [jnp.dot(a, weight_out, preferred_element_type=f32).astype(bf16) for a in active]
    outs = jnp.stack(outs, axis=1)
    total = add(lax.all_to_all(outs.reshape(4, quarter, width), ALL, 0, 0, axis_index_groups=near))
    parts = lax.all_to_all(total.astype(bf16).reshape(members, own, width), ALL, 0, 0, axis_index_groups=far)
    return (jnp.sum(parts.astype(f32), axis=0) + bias_out).astype(bf16)


def solution(mesh):
    in_specs = (
        P(("rows", "cols"), "depth"),
        P("depth", ("rows", "cols")),
        P(("rows", "cols")),
        P(("rows", "cols"), "depth"),
        P("depth"),
    )
    out_specs = P(("rows", "cols"), "depth")
    return jax.shard_map(shards, mesh=mesh, in_specs=in_specs, out_specs=out_specs, check_vma=False)
```
